32 devices in a mesh: dom: 16 (over z, y, core), grp: 2 (over x).
Axes of the slice: x: 2, y: 2, z: 4, core: 2. Of those that a mesh axis runs over, the one named last changes fastest.
Arguments:
- positions: float32 [3, 4096], P(None, ('dom', 'grp')), may hold values from 0 to 1
- features: bfloat16 [128, 4096], P(None, ('dom', 'grp')), may hold values from -6 to 6
- neighbour_weight: bfloat16 [128, 128], replicated, may hold values from -0.5 to 0.5
- adjoint: bfloat16 [256, 4096], P(None, ('dom', 'grp')), may hold values from -0.119628906 to 0.119628906
- basis_weight: bfloat16 [8, 128], replicated, may hold values from -2 to 2
- edge_weight: bfloat16 [128, 64], replicated, may hold values from -0.5 to 0.5
- tile_center: int32 [128], P(('dom', 'grp')), may hold values from 0 to 1
- tile_neighbour: int32 [128], P(('dom', 'grp')), may hold values from 0 to 5, as said below
- tile_count: int32 [32], P(('dom', 'grp')), may hold values from 2 to 4, as said below
Outputs:
- position_grad: float32 [3, 4096], P(None, ('dom', 'grp'))
The draws below stay inside these ranges and needn't reach their ends.
Inputs may be any that keep to these rules, and one draw needn't show every extreme that they name: `tile_count`: some device has all 4 slots live in every draw. `tile_neighbour`: the first slot of every device with an even index s names a block of the lower domain, that of every odd device a block of the upper domain; other slots are uniform over the three domains.
All inputs are finite; a program needn't handle non-finite values.
Results may differ from the reference program's by a relative error of at most 0.0012.
Values may be sent and summed in bfloat16 or wider, within the bound.
No kernel may reach another device: no remote copies, remote signals or barrier semaphores. Data moves between devices by JAX's collectives and lax.ppermute only.
A program may use at most 64 MiB of HBM per device.

```python
import jax
import jax.numpy as jnp
from jax import lax

LAT = 128
CH = 64
NB = 8
BLK = 128
BLK_DEV = 1
TILES_DEV = 4
SHARDS = 32
ATOMS = 4096
GROUP_BLOCKS = 2
TILE_SLOTS = 128
N_DOM = 16
N_GRP = 2


def draw_tile_count(key, part):
    first_key, second_key = jax.random.split(key)
    counts = jax.random.randint(first_key, (SHARDS,), (TILES_DEV + 1) // 2, TILES_DEV + 1)
    busiest = jax.random.randint(second_key, (), 0, SHARDS)
    return jnp.where(jnp.arange(SHARDS) == busiest, TILES_DEV, counts).astype(jnp.int32)


def draw_tile_neighbour(key, part):
    first_key = jax.random.fold_in(key, 11)
    second_key = jax.random.fold_in(key, 12)
    anywhere = jax.random.randint(first_key, (TILE_SLOTS,), 0, 3 * GROUP_BLOCKS)
    block_pick = jax.random.randint(second_key, (TILE_SLOTS,), 0, GROUP_BLOCKS)
    slots = jnp.arange(TILE_SLOTS, dtype=jnp.int32)
    device = slots // TILES_DEV
    slab_pick = 2 * (device % 2)
    first_slot = slots % TILES_DEV == 0
    return jnp.where(first_slot, slab_pick * GROUP_BLOCKS + block_pick, anywhere).astype(jnp.int32)


def touch_ends(values, key, smallest, high):
    dims = values.shape
    place = [jax.random.randint(jax.random.fold_in(key, axis), (), 0, dims[axis]) for axis in range(len(dims))]
    values = values.at[tuple(place)].set(smallest)
    longest = dims.index(max(dims))
    place[longest] = (place[longest] + 1) % dims[longest]
    return values.at[tuple(place)].set(high)


def block_scale(stream_key, shape, cuts, least, high):
    loudness, own = 1.0, jax.random.fold_in(stream_key, 6)
    for dim, parts in cuts:
        heights = jnp.exp(jax.random.uniform(jax.random.fold_in(own, dim), (parts,), jnp.float32, least / len(cuts), high / len(cuts)))
        loudness = loudness * jnp.repeat(heights, shape[dim] // parts).reshape([-1 if axis == dim else 1 for axis in range(len(shape))])
    return loudness


def gaussian(key, shape, width, reach, cuts=(), held_as=jnp.bfloat16):
    factor_of = block_scale(key, shape, cuts, -0.22, 0.18) if cuts else 1.0
    array = jax.random.normal(key, shape, jnp.float32) * width * factor_of
    return jnp.minimum(jnp.maximum(array, -reach), reach).astype(held_as)


def setup_inputs(seed: int = 0) -> dict:
    arg_keys = jax.random.split(jax.random.key(seed), 10)
    positions = jnp.clip(1.0 * jax.random.uniform(arg_keys[0], (3, ATOMS), jnp.float32) ** block_scale(arg_keys[0], (3, ATOMS), ((1, 32),), -0.2, 0.2), 0.0, 1.0)
    features = gaussian(arg_keys[1], (LAT, ATOMS), 1.0, 6.0, ((1, 32),))
    neighbour_weight = gaussian(arg_keys[2], (LAT, LAT), LAT ** -0.5, 0.5)
    adjoint = gaussian(arg_keys[3], (4 * CH, ATOMS), 0.02, 0.119628906, ((1, 32),))
    basis_weight = gaussian(arg_keys[4], (NB, LAT), NB ** -0.5, 2.0)
    edge_weight = gaussian(arg_keys[5], (LAT, CH), LAT ** -0.5, 0.5)
    tile_center = touch_ends(jax.random.randint(arg_keys[6], (TILE_SLOTS,), 0, GROUP_BLOCKS), jax.random.fold_in(arg_keys[6], 1), 0, GROUP_BLOCKS - 1).astype(jnp.int32)
    tile_neighbour = draw_tile_neighbour(jax.random.fold_in(arg_keys[9], 71), 0)
    tile_count = draw_tile_count(jax.random.fold_in(arg_keys[9], 71), 0)
    return dict(positions=positions, features=features, neighbour_weight=neighbour_weight, adjoint=adjoint, basis_weight=basis_weight, edge_weight=edge_weight, tile_center=tile_center, tile_neighbour=tile_neighbour, tile_count=tile_count)


slab_length = 1.0
cutoff_square = 4.0


def decay_rates(basis_count):
    return 0.3 * 1.5 ** jnp.arange(basis_count, dtype=jnp.float32)


def tile_terms(center_pos, neigh_pos, center_feat, neigh_feat, adj_center, basis_weight, edge_weight, self_pair):
    block_size = center_pos.shape[1]
    latent = center_feat.shape[0]
    channels = edge_weight.shape[1]
    basis_count = basis_weight.shape[0]
    displace = neigh_pos[:, None, :] - center_pos[:, :, None]
    dist_sq = jnp.sum(displace * displace, axis=0)
    identity = jnp.eye(block_size, dtype=jnp.float32)
    keep_mask = 1.0 - self_pair * identity
    inner_part = jnp.maximum(1.0 - dist_sq / cutoff_square, 0.0)
    envelope = inner_part * inner_part * keep_mask
    basis_rates = decay_rates(basis_count)
    basis_vals = jnp.exp(-dist_sq[:, :, None] * basis_rates)
    basis_low = basis_vals.astype(jnp.bfloat16)
    pre_act = jnp.dot(basis_low.reshape(-1, basis_count), basis_weight, preferred_element_type=jnp.float32).reshape(block_size, block_size, latent)
    pre_act = pre_act + center_feat.T.astype(jnp.float32)[:, None, :] + neigh_feat.T.astype(jnp.float32)[None, :, :]
    sigmoid_pre = jax.nn.sigmoid(pre_act)
    hidden = (pre_act * sigmoid_pre).astype(jnp.bfloat16)
    weights = jnp.dot(hidden.reshape(-1, latent), edge_weight, preferred_element_type=jnp.float32).reshape(block_size, block_size, channels)
    harmonics = jnp.concatenate([jnp.ones((1, block_size, block_size), jnp.float32), displace * 0.5], axis=0)
    adj_full = adj_center.astype(jnp.float32).reshape(4, channels, block_size)
    projected = jnp.einsum('mci,mij->ijc', adj_full, harmonics)
    gate_grad = (envelope[:, :, None] * projected).astype(jnp.bfloat16)
    along_chan = jnp.einsum('mci,ijc->mij', adj_full, weights)
    harm_grad = envelope[None] * along_chan
    env_grad = jnp.sum(along_chan * harmonics, axis=0)
    hidden_grad = lax.dot_general(gate_grad.reshape(-1, channels), edge_weight, (((1,), (1,)), ((), ())), preferred_element_type=jnp.float32).reshape(block_size, block_size, latent)
    pre_grad = (hidden_grad * sigmoid_pre * (1.0 + pre_act * (1.0 - sigmoid_pre))).astype(jnp.bfloat16)
    basis_grad = lax.dot_general(pre_grad.reshape(-1, latent), basis_weight, (((1,), (1,)), ((), ())), preferred_element_type=jnp.float32).reshape(block_size, block_size, basis_count)
    sq_grad = jnp.sum(basis_grad * basis_vals * (-basis_rates), axis=2) - env_grad * keep_mask * 2.0 * inner_part / cutoff_square
    disp_grad = 2.0 * sq_grad[None] * displace + 0.5 * harm_grad[1:]
    return -jnp.sum(disp_grad, axis=2), jnp.sum(disp_grad, axis=1)


def reference(positions, features, neighbour_weight, adjoint, basis_weight, edge_weight, tile_center, tile_neighbour, tile_count):
    neigh_all = lax.dot_general(neighbour_weight, features, (((0,), (0,)), ((), ())), preferred_element_type=jnp.float32).astype(jnp.bfloat16)
    group_blocks = BLK_DEV * N_GRP

    def tile_step(grad_total, tile_slot):
        device = tile_slot // TILES_DEV
        domain = device // N_GRP
        live_tile = (tile_slot % TILES_DEV < tile_count[device]).astype(jnp.float32)
        center = tile_center[tile_slot]
        neigh_block = tile_neighbour[tile_slot]
        slab_index = neigh_block // group_blocks - 1
        other_dom = jnp.mod(domain + slab_index, N_DOM)
        center_start = ((domain * group_blocks + center) * BLK).astype(jnp.int32)
        neigh_start = ((other_dom * group_blocks + neigh_block % group_blocks) * BLK).astype(jnp.int32)
        zero_row = jnp.zeros((), jnp.float32)
        lift_vec = jnp.stack([zero_row, zero_row, slab_index.astype(jnp.float32) * slab_length])[:, None]
        center_pos = lax.dynamic_slice_in_dim(positions, center_start, BLK, 1)
        neigh_pos = lax.dynamic_slice_in_dim(positions, neigh_start, BLK, 1) + lift_vec
        center_feat = lax.dynamic_slice_in_dim(features, center_start, BLK, 1)
        neigh_feat = lax.dynamic_slice_in_dim(neigh_all, neigh_start, BLK, 1)
        adj_center = lax.dynamic_slice_in_dim(adjoint, center_start, BLK, 1)
        self_pair = (neigh_block == center + group_blocks).astype(jnp.float32)
        center_grad, neigh_grad = tile_terms(center_pos, neigh_pos, center_feat, neigh_feat, adj_center, basis_weight, edge_weight, self_pair)
        old_center = lax.dynamic_slice_in_dim(grad_total, center_start, BLK, 1)
        grad_total = lax.dynamic_update_slice_in_dim(grad_total, old_center + live_tile * center_grad, center_start, 1)
        old_neigh = lax.dynamic_slice_in_dim(grad_total, neigh_start, BLK, 1)
        grad_total = lax.dynamic_update_slice_in_dim(grad_total, old_neigh + live_tile * neigh_grad, neigh_start, 1)
        return grad_total, None

    start_total = jnp.zeros((3, ATOMS), jnp.float32)
    grad_total, unused = lax.scan(tile_step, start_total, jnp.arange(TILE_SLOTS, dtype=jnp.int32))
    return grad_total
```

```python
import functools
import math

import jax
import jax.numpy as jnp
from jax import lax
from jax.experimental import pallas as pl
from jax.experimental.pallas import tpu as pltpu
from jax.sharding import PartitionSpec as P

slab_length = 1.0
cutoff_square = 4.0
F32 = jnp.float32
BF16 = jnp.bfloat16
COLUMN_STEP = 8
PAD_ROWS = 16


def turned(value, by):
    count = lax.axis_size("grp")
    return lax.ppermute(value, "grp", [((i + by) % count, i) for i in range(count)])


def swapped(value, side):
    count = lax.axis_size("dom")
    pairs = []
    for i in range(0, count, 2):
        other = (i + 1 - 2 * side) % count
        pairs += [(i, other), (other, i)]
    return lax.ppermute(value, "dom", pairs)


def pack_kernel(
    positions, features, adjoint, tile_center, tile_neighbour, tile_count, packed, whole, coords,
    lists, counts, sems,
):
    latent, block = features.shape
    slots = tile_center.shape[0]
    copies = [
        pltpu.make_async_copy(source, target, sems.at[n])
        for n, (source, target) in enumerate(
            [
                (features, packed.at[0:latent]),
                (features, whole.at[0:latent]),
                (adjoint, whole.at[latent + PAD_ROWS : whole.shape[0]]),
                (positions, coords),
                (tile_center, lists.at[0]),
                (tile_neighbour, lists.at[1]),
                (tile_count, counts),
            ]
        )
    ]
    for copy in copies:
        copy.start()
    for copy in copies[3:]:
        copy.wait()
    values = coords[...]
    high = values.astype(BF16).astype(F32)
    rest = values - high
    middle = rest.astype(BF16).astype(F32)
    low = rest - middle
    lane = lax.broadcasted_iota(jnp.int32, (1, block), 1)
    listed = jnp.where(lane == 2 * slots, counts[0], 0)
    for slot in range(slots):
        listed = jnp.where(lane == slot, lists[0, slot], listed)
        listed = jnp.where(lane == slots + slot, lists[1, slot], listed)
    parts = [high, middle, low, listed.astype(F32), jnp.zeros((PAD_ROWS - 10, block), F32)]
    parts = jnp.concatenate(parts, axis=0).astype(BF16)
    packed[latent : latent + PAD_ROWS, :] = parts
    whole[latent : latent + PAD_ROWS, :] = parts
    for copy in copies[:3]:
        copy.wait()


def tiles_kernel(groups, slots, far, listed_far, own, side, weights, earlier, results, scratch):
    (neighbour_weight, basis_weight, edge_weight) = weights
    (half_neigh, pos, half_own, dist, env_harm, displace, keep_inner, radial, along, listed,
     listed_smem, sem, tally, work, *extra) = scratch
    if far:
        mixed, cols, _, earlier_neigh = earlier
        *shares, far_out, near_out, own_sums = results
        neigh_sums = extra[0]
    else:
        mixed, cols, own_sums, neigh_sums, far_work = results
    latent, block = neighbour_weight.shape
    basis_count = basis_weight.shape[0]
    channels = edge_weight.shape[0]
    rows = block // groups
    packed_rows = latent + PAD_ROWS
    window = 3 * groups
    member = lax.axis_index("grp")
    near_slab = 2 - 2 * lax.rem(lax.axis_index("dom"), 2)
    far_slab = 2 - near_slab
    side_slab = far_slab if far else near_slab

    if not far:
        for turn in range(groups):
            row = own[turn][latent : latent + PAD_ROWS, :].astype(F32)[8:16, :]
            listed[turn * 8 : turn * 8 + 8, :] = row.astype(jnp.int32)
        to_scalars = pltpu.make_async_copy(listed, listed_smem, sem)
        to_scalars.start()

    third = lax.broadcasted_iota(jnp.int32, (8, block), 0) == 2
    zero5 = jnp.zeros((5, block), F32)

    def coords_of(part):
        return jnp.concatenate([part[0:3] + part[3:6] + part[6:9], zero5], axis=0)

    def neighbour(index, ref, start, lift):
        product = lax.dot_general(
            neighbour_weight[...],
            ref[start : start + latent, :],
            (((0,), (0,)), ((), ())),
            preferred_element_type=F32,
        )
        half_neigh[index] = product.astype(BF16) * 0.5
        part = ref[start + latent : start + packed_rows, :].astype(F32)
        pos[index] = coords_of(part) + jnp.where(third, lift, 0.0)

    lift = jnp.asarray(side_slab - 1, jnp.int32).astype(F32) * slab_length
    neighbour(groups, side, 0, lift)
    if not far:
        for turn in range(groups):
            neighbour(turn, own[turn], 0, 0.0)

    sub8 = lax.broadcasted_iota(jnp.int32, (8, block), 0)
    rates = jnp.zeros((8, block), F32)
    for b in range(basis_count):
        rates = jnp.where(sub8 == b, 0.3 * 1.5**b, rates)
    weight_rows = basis_weight[...].astype(F32) * 0.5
    rated_rows = weight_rows * rates
    exponents = rates * (-math.log2(math.e))
    lane = lax.broadcasted_iota(jnp.int32, (latent, block), 1)
    weight_cols = (
        jnp.concatenate([weight_rows, jnp.zeros((block - basis_count, latent), F32)], axis=0)
        .T[:, 0 : 2 * basis_count]
        .astype(BF16)
    )
    for turn in range(groups):
        half_own[turn] = own[turn][0:latent, :].astype(F32) * 0.5
        if far:
            continue
        own_sums[3 * turn : 3 * turn + 3] = jnp.zeros((3, block, block), F32)
        for m in range(4):
            at = (turn * 8 + m) * block
            mixed[at : at + block, :] = lax.dot_general(
                own[turn][packed_rows + m * channels : packed_rows + (m + 1) * channels, :],
                edge_weight[...],
                (((0,), (0,)), ((), ())),
                preferred_element_type=F32,
            )
            at = (turn * 8 + 4 + m) * block
            mixed[at : at + block, :] = jnp.zeros((block, latent), F32)
        part = own[turn][latent : latent + PAD_ROWS, :].astype(F32)
        column = jnp.concatenate(
            [coords_of(part), jnp.zeros((block - 8, block), F32)], axis=0
        ).T
        for axis in range(3):
            cols[turn * 3 + axis] = jnp.broadcast_to(column[:, axis : axis + 1], (block, block))
    neigh_sums[...] = jnp.zeros_like(neigh_sums)

    if not far:
        for entry in range(groups * window):
            tally[entry] = 0
        to_scalars.wait()
        for turn in range(groups):
            at = turn * 8 + 1
            count = listed_smem[at, 2 * slots]
            for slot in range(slots):
                entry = listed_smem[at, slot] * window + listed_smem[at, slots + slot]
                tally[entry] += jnp.where(slot < count, 1, 0)

        def copies_of(center, slab, b):
            return tally[center * window + slab * groups + b]

        def live(center, slab, b):
            return jnp.where(copies_of(center, slab, b) > 0, 1, 0)

        pool = sum(live(center, 1, b) for center in range(groups) for b in range(groups))
        fixed = [
            sum(live(center, slab, b) for center in range(groups) for slab in (0, 2))
            for b in range(groups)
        ]
        target = pool + sum(fixed)
        begin, end, edge = jnp.int32(0), jnp.int32(0), jnp.int32(0)
        for b in range(groups):
            following = jnp.minimum(
                edge + jnp.maximum(target - groups * fixed[b], 0), groups * pool
            )
            begin = jnp.where(member == b, edge, begin)
            end = jnp.where(member == b, following, end)
            edge = following
        units = jnp.int32(0)
        for center in range(groups):
            turn = lax.rem(center - member + groups, groups)
            work[0, units] = turn
            work[2, units] = groups
            work[3, units] = copies_of(center, near_slab, member)
            units = units + live(center, near_slab, member)
        whole_units = units
        place = jnp.int32(0)
        for center in range(groups):
            turn = lax.rem(center - member + groups, groups)
            for b in range(groups):
                for part in range(groups):
                    work[0, units] = turn
                    work[1, units] = part
                    work[2, units] = lax.rem(b - member + groups, groups)
                    work[3, units] = copies_of(center, 1, b)
                    mine = jnp.logical_and(place >= begin, place < end)
                    units = units + jnp.where(mine, live(center, 1, b), 0)
                    place = place + live(center, 1, b)
        far_units = jnp.int32(0)
        for center in range(groups):
            far_work[1 + far_units * 2] = lax.rem(center - member + groups, groups)
            far_work[2 + far_units * 2] = copies_of(center, far_slab, member)
            far_units = far_units + live(center, far_slab, member)
        far_work[0] = far_units
    else:
        units = whole_units = listed_far[0]

    def run_unit(rows, unit, carry):
        if far:
            center_turn = listed_far[1 + unit * 2]
            first_row = 0
            copies = listed_far[2 + unit * 2].astype(F32)
            index = groups
            self_pair = jnp.float32(0.0)
        else:
            center_turn = work[0, unit]
            first_row = pl.multiple_of(work[1, unit] * rows, rows) if rows < block else 0
            index = work[2, unit]
            copies = work[3, unit].astype(F32)
            self_pair = jnp.where(center_turn == index, 1.0, 0.0).astype(F32)

        square = None
        steps = []
        for axis in range(3):
            step = (
                pos[index, axis : axis + 1, :]
                - cols[center_turn * 3 + axis, pl.ds(first_row, rows), :]
            )
            steps.append(step)
            square = step * step if square is None else square + step * step
        same = (
            lax.broadcasted_iota(jnp.int32, (rows, block), 0) + first_row
            == lax.broadcasted_iota(jnp.int32, (rows, block), 1)
        )
        keep = 1.0 - self_pair * jnp.where(same, 1.0, 0.0)
        inner = jnp.maximum(1.0 - square * (1.0 / cutoff_square), 0.0) * keep
        envelope = inner * inner
        dist[0:rows, :] = square
        keep_inner[0:rows, :] = inner
        env_harm[0:rows, :] = envelope
        for axis in range(3):
            displace[axis, 0:rows, :] = steps[axis]
            env_harm[(axis + 1) * rows : (axis + 2) * rows, :] = envelope * (steps[axis] * 0.5)
        half_n = half_neigh[index]
        half_two = jnp.concatenate([half_n, half_n], axis=1)
        half_center = half_own[center_turn]

        for chunk in range(rows // COLUMN_STEP):
            first = chunk * COLUMN_STEP
            shift = lax.rem(2 * block - first_row - first + basis_count, block)
            rolled = pltpu.roll(half_center, shift, 1)[:, 0 : 2 * basis_count].astype(BF16)
            left = jnp.where(lane[:, 0 : 2 * basis_count] < basis_count, weight_cols, rolled)
            for k in range(0, COLUMN_STEP, 2):
                right = []
                basis = []
                for e in (k, k + 1):
                    vals = jnp.exp2(exponents * dist[first + e : first + e + 1, :])
                    basis.append(vals)
                    onehot = jnp.where(sub8 == e, 1.0, 0.0)
                    right.append(jnp.concatenate([vals, onehot], axis=0).astype(BF16))
                right = jnp.concatenate(right, axis=1)
                pre = jnp.dot(left, right, preferred_element_type=F32)
                half = pre.astype(BF16) + half_two
                tanh = jnp.tanh(half)
                up = 1 + tanh
                hidden = half * up
                slope = up + hidden * (1 - tanh)
                both = jnp.concatenate([slope, hidden], axis=0)
                lhs = []
                for e in (k, k + 1):
                    at = center_turn * (8 * block) + first_row + first + e
                    mix = [mixed[pl.ds(at + m * block, 1), :] for m in range(4)]
                    top = jnp.concatenate([mix[m] * rated_rows for m in range(4)], axis=0)
                    exact = mixed[pl.ds(at, 8, stride=block), :]
                    high = exact.astype(BF16).astype(F32)
                    low = jnp.concatenate([high, exact - high], axis=0)
                    lhs.append(
                        jnp.concatenate(
                            [
                                jnp.concatenate([top, jnp.zeros((16, latent), F32)], axis=0),
                                jnp.concatenate([jnp.zeros((32, latent), F32), low], axis=0),
                            ],
                            axis=1,
                        ).astype(BF16)
                    )
                outs = jnp.dot(jnp.concatenate(lhs, axis=0), both, preferred_element_type=F32)
                for n, e in enumerate((k, k + 1)):
                    row = first + e
                    out = outs[n * 48 : (n + 1) * 48, n * block : (n + 1) * block]
                    total = None
                    for m in range(4):
                        at = m * rows + row
                        term = env_harm[at : at + 1, :] * out[m * 8 : m * 8 + 8]
                        total = term if total is None else total + term
                    radial[row * 8 : row * 8 + 8, :] = total * basis[n]
                    along[row * 8 : row * 8 + 8, :] = out[32:40] + out[40:48]

        totals = [jnp.zeros((8, block), F32) for _ in range(3)]
        scale = copies * 2.0
        for part in range(rows // 8):
            at = slice(part * 8, part * 8 + 8)
            basis_part = None
            for b in range(basis_count):
                term = radial[pl.ds(part * 64 + b, 8, stride=8), :]
                basis_part = term if basis_part is None else basis_part + term
            alongs = [along[pl.ds(part * 64 + m, 8, stride=8), :] for m in range(4)]
            step = [displace[axis, at, :] for axis in range(3)]
            env_grad = alongs[0] + 0.5 * (
                alongs[1] * step[0] + alongs[2] * step[1] + alongs[3] * step[2]
            )
            square_grad = -basis_part - env_grad * keep_inner[at, :] * (2.0 / cutoff_square)
            half_env = (0.5 * copies) * env_harm[at, :]
            square_grad = scale * square_grad
            at_center = pl.ds(pl.multiple_of(first_row + part * 8, 8), 8)
            for axis in range(3):
                grad = square_grad * step[axis] + half_env * alongs[axis + 1]
                totals[axis] = totals[axis] + grad
                own_sums[center_turn * 3 + axis, at_center, :] += grad
        for axis in range(3):
            neigh_sums[3 * index + axis] += totals[axis]
        return carry

    lax.fori_loop(0, whole_units, functools.partial(run_unit, block), 0)
    if not far:
        lax.fori_loop(whole_units, units, functools.partial(run_unit, rows), 0)
    if not far:
        return

    def column_sums(ref, index):
        return jnp.concatenate(
            [jnp.sum(ref[3 * index + axis], axis=0, keepdims=True) for axis in range(3)], axis=0
        )

    far_out[...] = column_sums(neigh_sums, groups)
    near_out[...] = column_sums(earlier_neigh, groups)
    for turn in range(groups):
        wide = jnp.zeros((block, block), F32)
        for axis in range(3):
            rows_sum = jnp.sum(own_sums[3 * turn + axis], axis=1, keepdims=True)
            wide = jnp.where(lane == axis, rows_sum, wide)
        shares[turn][...] = column_sums(earlier_neigh, turn) - wide.T[0:3, :]


def tiles_call(groups, slots, far, listed_far, own, side, weights, earlier):
    latent, block = weights[0].shape
    rows = block // groups
    vmem = pl.BlockSpec(memory_space=pltpu.VMEM)
    smem = pl.BlockSpec(memory_space=pltpu.SMEM)
    operands = [*own, side, *weights, *earlier]
    specs = [vmem] * len(operands)
    sums_shape = (3 * groups, block, block)
    if far:
        results = [jax.ShapeDtypeStruct((3, block), F32)] * (groups + 2)
        results.append(pltpu.VMEM(sums_shape, F32))
        operands = [listed_far] + operands
        specs = [smem] + specs
    else:
        shapes = [(8 * groups * block, latent), sums_shape, sums_shape, (3 * (groups + 1), 8, block)]
        results = [pltpu.VMEM(shape, F32) for shape in shapes]
        results.append(pltpu.SMEM((1 + 2 * (groups + 1),), jnp.int32))
    result_specs = [vmem] * len(results)
    if not far:
        result_specs[-1] = smem

    def body(*refs):
        refs = list(refs)
        take = lambda count: [refs.pop(0) for _ in range(count)]
        listed_ref = take(1)[0] if far else None
        own_refs = take(groups)
        (side_ref,) = take(1)
        weight_refs = take(3)
        earlier_refs = take(len(earlier))
        result_refs = take(len(results))
        tiles_kernel(
            groups, slots, far, listed_ref, own_refs, side_ref, weight_refs, earlier_refs,
            result_refs, refs,
        )

    tiles = groups * slots // (3 if far else 2)
    return pl.pallas_call(
        body,
        out_shape=results,
        in_specs=specs,
        out_specs=result_specs,
        input_output_aliases={len(operands) - 2: groups + 2} if far else {},
        scratch_shapes=[
            pltpu.VMEM((groups + 1, latent, block), BF16),
            pltpu.VMEM((groups + 1, 8, block), F32),
            pltpu.VMEM((groups, latent, block), F32),
            pltpu.VMEM((block, block), F32),
            pltpu.VMEM((4 * block, block), F32),
            pltpu.VMEM((3, block, block), F32),
            pltpu.VMEM((block, block), F32),
            pltpu.VMEM((8 * block, block), F32),
            pltpu.VMEM((8 * block, block), F32),
            pltpu.VMEM((8 * groups, block), jnp.int32),
            pltpu.SMEM((8 * groups, block), jnp.int32),
            pltpu.SemaphoreType.DMA,
            pltpu.SMEM((3 * groups * groups,), jnp.int32),
            pltpu.SMEM((4, groups * groups * (groups + 1) + 1), jnp.int32),
        ]
        + ([pltpu.VMEM((3 * (groups + 1), 8, block), F32)] if far else []),
        compiler_params=pltpu.CompilerParams(vmem_limit_bytes=32 * 1024 * 1024),
        cost_estimate=pl.CostEstimate(
            flops=tiles * rows * block * latent * 200,
            bytes_accessed=sum(x.size * x.dtype.itemsize for x in operands),
            transcendentals=tiles * rows * block * latent,
        ),
        name="far_tiles" if far else "near_tiles",
    )(*operands)


def on_device(
    positions,
    features,
    neighbour_weight,
    adjoint,
    basis_weight,
    edge_weight,
    tile_center,
    tile_neighbour,
    tile_count,
):
    groups = lax.axis_size("grp")
    latent, block = features.shape
    slots = tile_center.shape[0]
    packed_rows = latent + PAD_ROWS
    packed, whole = pl.pallas_call(
        pack_kernel,
        out_shape=[
            pltpu.VMEM((packed_rows, block), BF16),
            pltpu.VMEM((packed_rows + adjoint.shape[0], block), BF16),
        ],
        in_specs=[pl.BlockSpec(memory_space=pl.ANY)] * 6,
        out_specs=[pl.BlockSpec(memory_space=pltpu.VMEM)] * 2,
        scratch_shapes=[
            pltpu.VMEM(positions.shape, F32),
            pltpu.SMEM((2, slots), jnp.int32),
            pltpu.SMEM((1,), jnp.int32),
            pltpu.SemaphoreType.DMA((7,)),
        ],
        name="pack_rows",
    )(positions, features, adjoint, tile_center, tile_neighbour, tile_count)
    own = [whole] + [turned(whole, turn) for turn in range(1, groups)]
    near = swapped(packed, 0)
    far = swapped(packed, 1)
    weights = (neighbour_weight, basis_weight, edge_weight.T)
    *kept, far_work = tiles_call(groups, slots, False, None, own, near, weights, [])
    *shares, far_sum, near_sum, _ = tiles_call(
        groups, slots, True, far_work, own, far, weights, kept
    )
    total = shares[0] + swapped(far_sum, 1) + swapped(near_sum, 0)
    for turn in range(1, groups):
        total = total + turned(shares[turn], -turn)
    return total


def solution(mesh):
    placed = (
        P(None, ("dom", "grp")),
        P(None, ("dom", "grp")),
        P(),
        P(None, ("dom", "grp")),
        P(),
        P(),
        P(("dom", "grp")),
        P(("dom", "grp")),
        P(("dom", "grp")),
    )
    return jax.shard_map(
        on_device, mesh=mesh, in_specs=placed, out_specs=P(None, ("dom", "grp")), check_vma=False
    )
```

```python
import functools
import math

import jax
import jax.numpy as jnp
from jax import lax
from jax.experimental import pallas as pl
from jax.experimental.pallas import tpu as pltpu
from jax.sharding import PartitionSpec as P

slab_length = 1.0
cutoff_square = 4.0
F32 = jnp.float32
BF16 = jnp.bfloat16
COLUMN_STEP = 8
PAD_ROWS = 16


def turned(value, by):
    count = lax.axis_size("grp")
    return lax.ppermute(value, "grp", [((i + by) % count, i) for i in range(count)])


def swapped(value, side):
    count = lax.axis_size("dom")
    pairs = []
    for i in range(0, count, 2):
        other = (i + 1 - 2 * side) % count
        pairs += [(i, other), (other, i)]
    return lax.ppermute(value, "dom", pairs)


def pack_kernel(
    positions, features, adjoint, tile_center, tile_neighbour, tile_count, packed, whole, coords,
    lists, counts, sems,
):
    latent, block = features.shape
    slots = tile_center.shape[0]
    copies = [
        pltpu.make_async_copy(source, target, sems.at[n])
        for n, (source, target) in enumerate(
            [
                (features, packed.at[0:latent]),
                (features, whole.at[0:latent]),
                (adjoint, whole.at[latent + PAD_ROWS : whole.shape[0]]),
                (positions, coords),
                (tile_center, lists.at[0]),
                (tile_neighbour, lists.at[1]),
                (tile_count, counts),
            ]
        )
    ]
    for copy in copies:
        copy.start()
    for copy in copies[3:]:
        copy.wait()
    values = coords[...]
    high = values.astype(BF16).astype(F32)
    rest = values - high
    middle = rest.astype(BF16).astype(F32)
    low = rest - middle
    lane = lax.broadcasted_iota(jnp.int32, (1, block), 1)
    listed = jnp.where(lane == 2 * slots, counts[0], 0)
    for slot in range(slots):
        listed = jnp.where(lane == slot, lists[0, slot], listed)
        listed = jnp.where(lane == slots + slot, lists[1, slot], listed)
    parts = [high, middle, low, listed.astype(F32), jnp.zeros((PAD_ROWS - 10, block), F32)]
    parts = jnp.concatenate(parts, axis=0).astype(BF16)
    packed[latent : latent + PAD_ROWS, :] = parts
    whole[latent : latent + PAD_ROWS, :] = parts
    for copy in copies[:3]:
        copy.wait()


def tiles_kernel(groups, slots, far, listed_far, own, side, weights, earlier, results, scratch):
    (neighbour_weight, basis_weight, edge_weight) = weights
    (half_neigh, pos, half_own, dist, env_harm, displace, keep_inner, radial, along, listed,
     listed_smem, sem, tally, work, *extra) = scratch
    if far:
        mixed, cols, _, earlier_neigh = earlier
        *shares, far_out, near_out, own_sums = results
        neigh_sums = extra[0]
    else:
        mixed, cols, own_sums, neigh_sums, far_work = results
    latent, block = neighbour_weight.shape
    basis_count = basis_weight.shape[0]
    channels = edge_weight.shape[0]
    rows = block // groups
    packed_rows = latent + PAD_ROWS
    window = 3 * groups
    member = lax.axis_index("grp")
    near_slab = 2 - 2 * lax.rem(lax.axis_index("dom"), 2)
    far_slab = 2 - near_slab
    side_slab = far_slab if far else near_slab

    if not far:
        for turn in range(groups):
            row = own[turn][latent : latent + PAD_ROWS, :].astype(F32)[8:16, :]
            listed[turn * 8 : turn * 8 + 8, :] = row.astype(jnp.int32)
        to_scalars = pltpu.make_async_copy(listed, listed_smem, sem)
        to_scalars.start()

    third = lax.broadcasted_iota(jnp.int32, (8, block), 0) == 2
    zero5 = jnp.zeros((5, block), F32)

    def coords_of(part):
        return jnp.concatenate([part[0:3] + part[3:6] + part[6:9], zero5], axis=0)

    def neighbour(index, ref, start, lift):
        product = lax.dot_general(
            neighbour_weight[...],
            ref[start : start + latent, :],
            (((0,), (0,)), ((), ())),
            preferred_element_type=F32,
        )
        half_neigh[index] = product.astype(BF16) * 0.5
        part = ref[start + latent : start + packed_rows, :].astype(F32)
        pos[index] = coords_of(part) + jnp.where(third, lift, 0.0)

    lift = jnp.asarray(side_slab - 1, jnp.int32).astype(F32) * slab_length
    neighbour(groups, side, 0, lift)
    if not far:
        for turn in range(groups):
            neighbour(turn, own[turn], 0, 0.0)

    sub8 = lax.broadcasted_iota(jnp.int32, (8, block), 0)
    rates = jnp.zeros((8, block), F32)
    for b in range(basis_count):
        rates = jnp.where(sub8 == b, 0.3 * 1.5**b, rates)
    weight_rows = basis_weight[...].astype(F32) * 0.5
    rated_rows = weight_rows * rates
    exponents = rates * (-math.log2(math.e))
    lane = lax.broadcasted_iota(jnp.int32, (latent, block), 1)
    weight_cols = (
        jnp.concatenate([weight_rows, jnp.zeros((block - basis_count, latent), F32)], axis=0)
        .T
    )
    eye = jnp.where(
        lax.broadcasted_iota(jnp.int32, (latent, latent), 0)
        == lax.broadcasted_iota(jnp.int32, (latent, latent), 1),
        1.0,
        0.0,
    ).astype(BF16)
    for turn in range(groups):
        half_own[turn] = own[turn][0:latent, :].astype(F32) * 0.5
        if far:
            continue
        own_sums[3 * turn : 3 * turn + 3] = jnp.zeros((3, block, block), F32)
        for m in range(4):
            at = (turn * 8 + m) * block
            mixed[at : at + block, :] = lax.dot_general(
                own[turn][packed_rows + m * channels : packed_rows + (m + 1) * channels, :],
                edge_weight[...],
                (((0,), (0,)), ((), ())),
                preferred_element_type=F32,
            )
            at = (turn * 8 + 4 + m) * block
            mixed[at : at + block, :] = jnp.zeros((block, latent), F32)
        part = own[turn][latent : latent + PAD_ROWS, :].astype(F32)
        column = jnp.concatenate(
            [coords_of(part), jnp.zeros((block - 8, block), F32)], axis=0
        ).T
        for axis in range(3):
            cols[turn * 3 + axis] = jnp.broadcast_to(column[:, axis : axis + 1], (block, block))
    neigh_sums[...] = jnp.zeros_like(neigh_sums)

    if not far:
        for entry in range(groups * window):
            tally[entry] = 0
        to_scalars.wait()
        for turn in range(groups):
            at = turn * 8 + 1
            count = listed_smem[at, 2 * slots]
            for slot in range(slots):
                entry = listed_smem[at, slot] * window + listed_smem[at, slots + slot]
                tally[entry] += jnp.where(slot < count, 1, 0)

        def copies_of(center, slab, b):
            return tally[center * window + slab * groups + b]

        def live(center, slab, b):
            return jnp.where(copies_of(center, slab, b) > 0, 1, 0)

        pool = sum(live(center, 1, b) for center in range(groups) for b in range(groups))
        fixed = [
            sum(live(center, slab, b) for center in range(groups) for slab in (0, 2))
            for b in range(groups)
        ]
        target = pool + sum(fixed)
        begin, end, edge = jnp.int32(0), jnp.int32(0), jnp.int32(0)
        for b in range(groups):
            following = jnp.minimum(
                edge + jnp.maximum(target - groups * fixed[b], 0), groups * pool
            )
            begin = jnp.where(member == b, edge, begin)
            end = jnp.where(member == b, following, end)
            edge = following
        units = jnp.int32(0)
        for center in range(groups):
            turn = lax.rem(center - member + groups, groups)
            work[0, units] = turn
            work[2, units] = groups
            work[3, units] = copies_of(center, near_slab, member)
            units = units + live(center, near_slab, member)
        whole_units = units
        place = jnp.int32(0)
        for center in range(groups):
            turn = lax.rem(center - member + groups, groups)
            for b in range(groups):
                for part in range(groups):
                    work[0, units] = turn
                    work[1, units] = part
                    work[2, units] = lax.rem(b - member + groups, groups)
                    work[3, units] = copies_of(center, 1, b)
                    mine = jnp.logical_and(place >= begin, place < end)
                    units = units + jnp.where(mine, live(center, 1, b), 0)
                    place = place + live(center, 1, b)
        far_units = jnp.int32(0)
        for center in range(groups):
            far_work[1 + far_units * 2] = lax.rem(center - member + groups, groups)
            far_work[2 + far_units * 2] = copies_of(center, far_slab, member)
            far_units = far_units + live(center, far_slab, member)
        far_work[0] = far_units
    else:
        units = whole_units = listed_far[0]

    def run_unit(rows, unit, carry):
        if far:
            center_turn = listed_far[1 + unit * 2]
            first_row = 0
            copies = listed_far[2 + unit * 2].astype(F32)
            index = groups
            self_pair = jnp.float32(0.0)
        else:
            center_turn = work[0, unit]
            first_row = pl.multiple_of(work[1, unit] * rows, rows) if rows < block else 0
            index = work[2, unit]
            copies = work[3, unit].astype(F32)
            self_pair = jnp.where(center_turn == index, 1.0, 0.0).astype(F32)

        square = None
        steps = []
        for axis in range(3):
            step = (
                pos[index, axis : axis + 1, :]
                - cols[center_turn * 3 + axis, pl.ds(first_row, rows), :]
            )
            steps.append(step)
            square = step * step if square is None else square + step * step
        same = (
            lax.broadcasted_iota(jnp.int32, (rows, block), 0) + first_row
            == lax.broadcasted_iota(jnp.int32, (rows, block), 1)
        )
        keep = 1.0 - self_pair * jnp.where(same, 1.0, 0.0)
        inner = jnp.maximum(1.0 - square * (1.0 / cutoff_square), 0.0) * keep
        envelope = inner * inner
        dist[0:rows, :] = square
        keep_inner[0:rows, :] = inner
        env_harm[0:rows, :] = envelope
        for axis in range(3):
            displace[axis, 0:rows, :] = steps[axis]
            env_harm[(axis + 1) * rows : (axis + 2) * rows, :] = envelope * (steps[axis] * 0.5)
        half_n = half_neigh[index]
        rest = jnp.concatenate([jnp.zeros((block - 2 * basis_count, block), BF16), half_n], axis=0)
        rest = jnp.concatenate([rest, rest], axis=1)
        half_center = half_own[center_turn]

        for chunk in range(rows // COLUMN_STEP):
            first = chunk * COLUMN_STEP
            shift = lax.rem(2 * block - first_row - first + basis_count, block)
            rolled = pltpu.roll(half_center, shift, 1)
            rolled = jnp.where(lane < basis_count, weight_cols, rolled)
            rolled = jnp.where(lane < 2 * basis_count, rolled, 0.0)
            left = jnp.concatenate([rolled.astype(BF16), eye], axis=1)
            for k in range(0, COLUMN_STEP, 2):
                right = []
                basis = []
                for e in (k, k + 1):
                    vals = jnp.exp2(exponents * dist[first + e : first + e + 1, :])
                    basis.append(vals)
                    onehot = jnp.where(sub8 == e, 1.0, 0.0)
                    right.append(jnp.concatenate([vals, onehot], axis=0).astype(BF16))
                right = jnp.concatenate([jnp.concatenate(right, axis=1), rest], axis=0)
                pre = jnp.dot(left, right, preferred_element_type=F32)
                for n, e in enumerate((k, k + 1)):
                    half = pre[:, n * block : (n + 1) * block].astype(BF16)
                    tanh = jnp.tanh(half)
                    up = 1 + tanh
                    hidden = half * up
                    slope = up + hidden * (1 - tanh)
                    both = jnp.concatenate([slope, hidden], axis=0)
                    row = first + e
                    at = center_turn * (8 * block) + first_row + row
                    mix = [mixed[pl.ds(at + m * block, 1), :] for m in range(4)]
                    top = jnp.concatenate([mix[m] * rated_rows for m in range(4)], axis=0)
                    exact = mixed[pl.ds(at, 8, stride=block), :]
                    high = exact.astype(BF16).astype(F32)
                    low = jnp.concatenate([high, exact - high], axis=0)
                    lhs = jnp.concatenate(
                        [
                            jnp.concatenate([top, jnp.zeros((16, latent), F32)], axis=0),
                            jnp.concatenate([jnp.zeros((32, latent), F32), low], axis=0),
                        ],
                        axis=1,
                    ).astype(BF16)
                    out = jnp.dot(lhs, both, preferred_element_type=F32)
                    total = None
                    for m in range(4):
                        at = m * rows + row
                        term = env_harm[at : at + 1, :] * out[m * 8 : m * 8 + 8]
                        total = term if total is None else total + term
                    radial[row * 8 : row * 8 + 8, :] = total * basis[n]
                    along[row * 8 : row * 8 + 8, :] = out[32:40] + out[40:48]

        totals = [jnp.zeros((8, block), F32) for _ in range(3)]
        scale = copies * 2.0
        for part in range(rows // 8):
            at = slice(part * 8, part * 8 + 8)
            basis_part = None
            for b in range(basis_count):
                term = radial[pl.ds(part * 64 + b, 8, stride=8), :]
                basis_part = term if basis_part is None else basis_part + term
            alongs = [along[pl.ds(part * 64 + m, 8, stride=8), :] for m in range(4)]
            step = [displace[axis, at, :] for axis in range(3)]
            env_grad = alongs[0] + 0.5 * (
                alongs[1] * step[0] + alongs[2] * step[1] + alongs[3] * step[2]
            )
            square_grad = -basis_part - env_grad * keep_inner[at, :] * (2.0 / cutoff_square)
            half_env = (0.5 * copies) * env_harm[at, :]
            square_grad = scale * square_grad
            at_center = pl.ds(pl.multiple_of(first_row + part * 8, 8), 8)
            for axis in range(3):
                grad = square_grad * step[axis] + half_env * alongs[axis + 1]
                totals[axis] = totals[axis] + grad
                own_sums[center_turn * 3 + axis, at_center, :] += grad
        for axis in range(3):
            neigh_sums[3 * index + axis] += totals[axis]
        return carry

    lax.fori_loop(0, whole_units, functools.partial(run_unit, block), 0)
    if not far:
        lax.fori_loop(whole_units, units, functools.partial(run_unit, rows), 0)
    if not far:
        return

    def column_sums(ref, index):
        return jnp.concatenate(
            [jnp.sum(ref[3 * index + axis], axis=0, keepdims=True) for axis in range(3)], axis=0
        )

    far_out[...] = column_sums(neigh_sums, groups)
    near_out[...] = column_sums(earlier_neigh, groups)
    for turn in range(groups):
        wide = jnp.zeros((block, block), F32)
        for axis in range(3):
            rows_sum = jnp.sum(own_sums[3 * turn + axis], axis=1, keepdims=True)
            wide = jnp.where(lane == axis, rows_sum, wide)
        shares[turn][...] = column_sums(earlier_neigh, turn) - wide.T[0:3, :]


def tiles_call(groups, slots, far, listed_far, own, side, weights, earlier):
    latent, block = weights[0].shape
    rows = block // groups
    vmem = pl.BlockSpec(memory_space=pltpu.VMEM)
    smem = pl.BlockSpec(memory_space=pltpu.SMEM)
    operands = [*own, side, *weights, *earlier]
    specs = [vmem] * len(operands)
    sums_shape = (3 * groups, block, block)
    if far:
        results = [jax.ShapeDtypeStruct((3, block), F32)] * (groups + 2)
        results.append(pltpu.VMEM(sums_shape, F32))
        operands = [listed_far] + operands
        specs = [smem] + specs
    else:
        shapes = [(8 * groups * block, latent), sums_shape, sums_shape, (3 * (groups + 1), 8, block)]
        results = [pltpu.VMEM(shape, F32) for shape in shapes]
        results.append(pltpu.SMEM((1 + 2 * (groups + 1),), jnp.int32))
    result_specs = [vmem] * len(results)
    if not far:
        result_specs[-1] = smem

    def body(*refs):
        refs = list(refs)
        take = lambda count: [refs.pop(0) for _ in range(count)]
        listed_ref = take(1)[0] if far else None
        own_refs = take(groups)
        (side_ref,) = take(1)
        weight_refs = take(3)
        earlier_refs = take(len(earlier))
        result_refs = take(len(results))
        tiles_kernel(
            groups, slots, far, listed_ref, own_refs, side_ref, weight_refs, earlier_refs,
            result_refs, refs,
        )

    tiles = groups * slots // (3 if far else 2)
    return pl.pallas_call(
        body,
        out_shape=results,
        in_specs=specs,
        out_specs=result_specs,
        input_output_aliases={len(operands) - 2: groups + 2} if far else {},
        scratch_shapes=[
            pltpu.VMEM((groups + 1, latent, block), BF16),
            pltpu.VMEM((groups + 1, 8, block), F32),
            pltpu.VMEM((groups, latent, block), F32),
            pltpu.VMEM((block, block), F32),
            pltpu.VMEM((4 * block, block), F32),
            pltpu.VMEM((3, block, block), F32),
            pltpu.VMEM((block, block), F32),
            pltpu.VMEM((8 * block, block), F32),
            pltpu.VMEM((8 * block, block), F32),
            pltpu.VMEM((8 * groups, block), jnp.int32),
            pltpu.SMEM((8 * groups, block), jnp.int32),
            pltpu.SemaphoreType.DMA,
            pltpu.SMEM((3 * groups * groups,), jnp.int32),
            pltpu.SMEM((4, groups * groups * (groups + 1) + 1), jnp.int32),
        ]
        + ([pltpu.VMEM((3 * (groups + 1), 8, block), F32)] if far else []),
        compiler_params=pltpu.CompilerParams(vmem_limit_bytes=32 * 1024 * 1024),
        cost_estimate=pl.CostEstimate(
            flops=tiles * rows * block * latent * 200,
            bytes_accessed=sum(x.size * x.dtype.itemsize for x in operands),
            transcendentals=tiles * rows * block * latent,
        ),
        name="far_tiles" if far else "near_tiles",
    )(*operands)


def on_device(
    positions,
    features,
    neighbour_weight,
    adjoint,
    basis_weight,
    edge_weight,
    tile_center,
    tile_neighbour,
    tile_count,
):
    groups = lax.axis_size("grp")
    latent, block = features.shape
    slots = tile_center.shape[0]
    packed_rows = latent + PAD_ROWS
    packed, whole = pl.pallas_call(
        pack_kernel,
        out_shape=[
            pltpu.VMEM((packed_rows, block), BF16),
            pltpu.VMEM((packed_rows + adjoint.shape[0], block), BF16),
        ],
        in_specs=[pl.BlockSpec(memory_space=pl.ANY)] * 6,
        out_specs=[pl.BlockSpec(memory_space=pltpu.VMEM)] * 2,
        scratch_shapes=[
            pltpu.VMEM(positions.shape, F32),
            pltpu.SMEM((2, slots), jnp.int32),
            pltpu.SMEM((1,), jnp.int32),
            pltpu.SemaphoreType.DMA((7,)),
        ],
        name="pack_rows",
    )(positions, features, adjoint, tile_center, tile_neighbour, tile_count)
    own = [whole] + [turned(whole, turn) for turn in range(1, groups)]
    near = swapped(packed, 0)
    far = swapped(packed, 1)
    weights = (neighbour_weight, basis_weight, edge_weight.T)
    *kept, far_work = tiles_call(groups, slots, False, None, own, near, weights, [])
    *shares, far_sum, near_sum, _ = tiles_call(
        groups, slots, True, far_work, own, far, weights, kept
    )
    total = shares[0] + swapped(far_sum, 1) + swapped(near_sum, 0)
    for turn in range(1, groups):
        total = total + turned(shares[turn], -turn)
    return total


def solution(mesh):
    placed = (
        P(None, ("dom", "grp")),
        P(None, ("dom", "grp")),
        P(),
        P(None, ("dom", "grp")),
        P(),
        P(),
        P(("dom", "grp")),
        P(("dom", "grp")),
        P(("dom", "grp")),
    )
    return jax.shard_map(
        on_device, mesh=mesh, in_specs=placed, out_specs=P(None, ("dom", "grp")), check_vma=False
    )
```

```python
import functools
import math

import jax
import jax.numpy as jnp
from jax import lax
from jax.experimental import pallas as pl
from jax.experimental.pallas import tpu as pltpu
from jax.sharding import PartitionSpec as P

slab_length = 1.0
cutoff_square = 4.0
F32 = jnp.float32
BF16 = jnp.bfloat16
COLUMN_STEP = 8
PAD_ROWS = 16


def turned(value, by):
    count = lax.axis_size("grp")
    return lax.ppermute(value, "grp", [((i + by) % count, i) for i in range(count)])


def swapped(value, side):
    count = lax.axis_size("dom")
    pairs = []
    for i in range(0, count, 2):
        other = (i + 1 - 2 * side) % count
        pairs += [(i, other), (other, i)]
    return lax.ppermute(value, "dom", pairs)


def pack_kernel(
    positions, features, adjoint, tile_center, tile_neighbour, tile_count, packed, whole, coords,
    lists, counts, sems,
):
    latent, block = features.shape
    slots = tile_center.shape[0]
    copies = [
        pltpu.make_async_copy(source, target, sems.at[n])
        for n, (source, target) in enumerate(
            [
                (features, packed.at[0:latent]),
                (features, whole.at[0:latent]),
                (adjoint, whole.at[latent + PAD_ROWS : whole.shape[0]]),
                (positions, coords),
                (tile_center, lists.at[0]),
                (tile_neighbour, lists.at[1]),
                (tile_count, counts),
            ]
        )
    ]
    for copy in copies:
        copy.start()
    for copy in copies[3:]:
        copy.wait()
    values = coords[...]
    high = values.astype(BF16).astype(F32)
    rest = values - high
    middle = rest.astype(BF16).astype(F32)
    low = rest - middle
    lane = lax.broadcasted_iota(jnp.int32, (1, block), 1)
    listed = jnp.where(lane == 2 * slots, counts[0], 0)
    for slot in range(slots):
        listed = jnp.where(lane == slot, lists[0, slot], listed)
        listed = jnp.where(lane == slots + slot, lists[1, slot], listed)
    parts = [high, middle, low, listed.astype(F32), jnp.zeros((PAD_ROWS - 10, block), F32)]
    parts = jnp.concatenate(parts, axis=0).astype(BF16)
    packed[latent : latent + PAD_ROWS, :] = parts
    whole[latent : latent + PAD_ROWS, :] = parts
    for copy in copies[:3]:
        copy.wait()


def tiles_kernel(groups, slots, stage, listed_far, own, side, weights, earlier, results, scratch):
    (neighbour_weight, basis_weight, edge_weight) = weights
    far = stage == "far"
    if far:
        mixed, cols, _, earlier_neigh, half_own = earlier
        *shares, far_out, near_out, own_sums = results
        (half_neigh, pos, neigh_sums, dist, env_harm, displace, keep_inner, radial, along) = scratch
    else:
        mixed, cols, own_sums, neigh_sums, half_own, half_neigh, pos, *far_work = results
        if stage == "near":
            (far_work,) = far_work
            (dist, env_harm, displace, keep_inner, radial, along, listed, listed_smem, sem, tally,
             work) = scratch
    prepared = {"ahead": range(1), "near": range(1, groups), "far": range(0)}[stage]
    latent, block = neighbour_weight.shape
    basis_count = basis_weight.shape[0]
    channels = edge_weight.shape[0]
    rows = block // groups
    packed_rows = latent + PAD_ROWS
    window = 3 * groups
    member = lax.axis_index("grp")
    near_slab = 2 - 2 * lax.rem(lax.axis_index("dom"), 2)
    far_slab = 2 - near_slab
    side_slab = far_slab if far else near_slab

    if stage == "near":
        for turn in range(groups):
            row = own[turn][latent : latent + PAD_ROWS, :].astype(F32)[8:16, :]
            listed[turn * 8 : turn * 8 + 8, :] = row.astype(jnp.int32)
        to_scalars = pltpu.make_async_copy(listed, listed_smem, sem)
        to_scalars.start()

    third = lax.broadcasted_iota(jnp.int32, (8, block), 0) == 2
    zero5 = jnp.zeros((5, block), F32)

    def coords_of(part):
        return jnp.concatenate([part[0:3] + part[3:6] + part[6:9], zero5], axis=0)

    def neighbour(index, ref, start, lift):
        product = lax.dot_general(
            neighbour_weight[...],
            ref[start : start + latent, :],
            (((0,), (0,)), ((), ())),
            preferred_element_type=F32,
        )
        half_neigh[index] = product.astype(BF16) * 0.5
        part = ref[start + latent : start + packed_rows, :].astype(F32)
        pos[index] = coords_of(part) + jnp.where(third, lift, 0.0)

    lift = jnp.asarray(side_slab - 1, jnp.int32).astype(F32) * slab_length
    if stage != "near":
        neighbour(groups, side, 0, lift)
    for turn in prepared:
        neighbour(turn, own[turn], 0, 0.0)

    sub8 = lax.broadcasted_iota(jnp.int32, (8, block), 0)
    rates = jnp.zeros((8, block), F32)
    for b in range(basis_count):
        rates = jnp.where(sub8 == b, 0.3 * 1.5**b, rates)
    weight_rows = basis_weight[...].astype(F32) * 0.5
    rated_rows = weight_rows * rates
    exponents = rates * (-math.log2(math.e))
    lane = lax.broadcasted_iota(jnp.int32, (latent, block), 1)
    weight_cols = (
        jnp.concatenate([weight_rows, jnp.zeros((block - basis_count, latent), F32)], axis=0)
        .T
    )
    eye = jnp.where(
        lax.broadcasted_iota(jnp.int32, (latent, latent), 0)
        == lax.broadcasted_iota(jnp.int32, (latent, latent), 1),
        1.0,
        0.0,
    ).astype(BF16)
    for turn in prepared:
        half_own[turn] = own[turn][0:latent, :].astype(F32) * 0.5
        own_sums[3 * turn : 3 * turn + 3] = jnp.zeros((3, block, block), F32)
        for m in range(4):
            at = (turn * 8 + m) * block
            mixed[at : at + block, :] = lax.dot_general(
                own[turn][packed_rows + m * channels : packed_rows + (m + 1) * channels, :],
                edge_weight[...],
                (((0,), (0,)), ((), ())),
                preferred_element_type=F32,
            )
            at = (turn * 8 + 4 + m) * block
            mixed[at : at + block, :] = jnp.zeros((block, latent), F32)
        part = own[turn][latent : latent + PAD_ROWS, :].astype(F32)
        column = jnp.concatenate(
            [coords_of(part), jnp.zeros((block - 8, block), F32)], axis=0
        ).T
        for axis in range(3):
            cols[turn * 3 + axis] = jnp.broadcast_to(column[:, axis : axis + 1], (block, block))
    if stage != "near":
        neigh_sums[...] = jnp.zeros_like(neigh_sums)
    if stage == "ahead":
        return

    if not far:
        for entry in range(groups * window):
            tally[entry] = 0
        to_scalars.wait()
        for turn in range(groups):
            at = turn * 8 + 1
            count = listed_smem[at, 2 * slots]
            for slot in range(slots):
                entry = listed_smem[at, slot] * window + listed_smem[at, slots + slot]
                tally[entry] += jnp.where(slot < count, 1, 0)

        def copies_of(center, slab, b):
            return tally[center * window + slab * groups + b]

        def live(center, slab, b):
            return jnp.where(copies_of(center, slab, b) > 0, 1, 0)

        pool = sum(live(center, 1, b) for center in range(groups) for b in range(groups))
        fixed = [
            sum(live(center, slab, b) for center in range(groups) for slab in (0, 2))
            for b in range(groups)
        ]
        target = pool + sum(fixed)
        begin, end, edge = jnp.int32(0), jnp.int32(0), jnp.int32(0)
        for b in range(groups):
            following = jnp.minimum(
                edge + jnp.maximum(target - groups * fixed[b], 0), groups * pool
            )
            begin = jnp.where(member == b, edge, begin)
            end = jnp.where(member == b, following, end)
            edge = following
        units = jnp.int32(0)
        for center in range(groups):
            turn = lax.rem(center - member + groups, groups)
            work[0, units] = turn
            work[2, units] = groups
            work[3, units] = copies_of(center, near_slab, member)
            units = units + live(center, near_slab, member)
        whole_units = units
        place = jnp.int32(0)
        for center in range(groups):
            turn = lax.rem(center - member + groups, groups)
            for b in range(groups):
                for part in range(groups):
                    work[0, units] = turn
                    work[1, units] = part
                    work[2, units] = lax.rem(b - member + groups, groups)
                    work[3, units] = copies_of(center, 1, b)
                    mine = jnp.logical_and(place >= begin, place < end)
                    units = units + jnp.where(mine, live(center, 1, b), 0)
                    place = place + live(center, 1, b)
        far_units = jnp.int32(0)
        for center in range(groups):
            far_work[1 + far_units * 2] = lax.rem(center - member + groups, groups)
            far_work[2 + far_units * 2] = copies_of(center, far_slab, member)
            far_units = far_units + live(center, far_slab, member)
        far_work[0] = far_units
    else:
        units = whole_units = listed_far[0]

    def run_unit(rows, unit, carry):
        if far:
            center_turn = listed_far[1 + unit * 2]
            first_row = 0
            copies = listed_far[2 + unit * 2].astype(F32)
            index = groups
            self_pair = jnp.float32(0.0)
        else:
            center_turn = work[0, unit]
            first_row = pl.multiple_of(work[1, unit] * rows, rows) if rows < block else 0
            index = work[2, unit]
            copies = work[3, unit].astype(F32)
            self_pair = jnp.where(center_turn == index, 1.0, 0.0).astype(F32)

        square = None
        steps = []
        for axis in range(3):
            step = (
                pos[index, axis : axis + 1, :]
                - cols[center_turn * 3 + axis, pl.ds(first_row, rows), :]
            )
            steps.append(step)
            square = step * step if square is None else square + step * step
        same = (
            lax.broadcasted_iota(jnp.int32, (rows, block), 0) + first_row
            == lax.broadcasted_iota(jnp.int32, (rows, block), 1)
        )
        keep = 1.0 - self_pair * jnp.where(same, 1.0, 0.0)
        inner = jnp.maximum(1.0 - square * (1.0 / cutoff_square), 0.0) * keep
        envelope = inner * inner
        dist[0:rows, :] = square
        keep_inner[0:rows, :] = inner
        env_harm[0:rows, :] = envelope
        for axis in range(3):
            displace[axis, 0:rows, :] = steps[axis]
            env_harm[(axis + 1) * rows : (axis + 2) * rows, :] = envelope * (steps[axis] * 0.5)
        half_n = half_neigh[index]
        rest = jnp.concatenate([jnp.zeros((block - 2 * basis_count, block), BF16), half_n], axis=0)
        rest = jnp.concatenate([rest, rest], axis=1)
        half_center = half_own[center_turn]

        for chunk in range(rows // COLUMN_STEP):
            first = chunk * COLUMN_STEP
            shift = lax.rem(2 * block - first_row - first + basis_count, block)
            rolled = pltpu.roll(half_center, shift, 1)
            rolled = jnp.where(lane < basis_count, weight_cols, rolled)
            rolled = jnp.where(lane < 2 * basis_count, rolled, 0.0)
            left = jnp.concatenate([rolled.astype(BF16), eye], axis=1)
            for k in range(0, COLUMN_STEP, 2):
                right = []
                basis = []
                for e in (k, k + 1):
                    vals = jnp.exp2(exponents * dist[pl.ds(first + e, 8, stride=0), :])
                    basis.append(vals)
                    onehot = jnp.where(sub8 == e, 1.0, 0.0)
                    right.append(jnp.concatenate([vals, onehot], axis=0).astype(BF16))
                right = jnp.concatenate([jnp.concatenate(right, axis=1), rest], axis=0)
                pre = jnp.dot(left, right, preferred_element_type=F32)
                for n, e in enumerate((k, k + 1)):
                    half = pre[:, n * block : (n + 1) * block].astype(BF16)
                    tanh = jnp.tanh(half)
                    up = 1 + tanh
                    hidden = half * up
                    slope = up + hidden * (1 - tanh)
                    both = jnp.concatenate([slope, hidden], axis=0)
                    row = first + e
                    at = center_turn * (8 * block) + first_row + row
                    mix = [mixed[pl.ds(at + m * block, 8, stride=0), :] for m in range(4)]
                    top = jnp.concatenate([mix[m] * rated_rows for m in range(4)], axis=0)
                    exact = mixed[pl.ds(at, 8, stride=block), :]
                    high = exact.astype(BF16).astype(F32)
                    low = jnp.concatenate([high, exact - high], axis=0)
                    lhs = jnp.concatenate(
                        [
                            jnp.concatenate([top, jnp.zeros((16, latent), F32)], axis=0),
                            jnp.concatenate([jnp.zeros((32, latent), F32), low], axis=0),
                        ],
                        axis=1,
                    ).astype(BF16)
                    out = jnp.dot(lhs, both, preferred_element_type=F32)
                    total = None
                    for m in range(4):
                        at = m * rows + row
                        term = env_harm[pl.ds(at, 8, stride=0), :] * out[m * 8 : m * 8 + 8]
                        total = term if total is None else total + term
                    radial[row * 8 : row * 8 + 8, :] = total * basis[n]
                    along[row * 8 : row * 8 + 8, :] = out[32:40] + out[40:48]

        totals = [jnp.zeros((8, block), F32) for _ in range(3)]
        scale = copies * 2.0
        for part in range(rows // 8):
            at = slice(part * 8, part * 8 + 8)
            basis_part = None
            for b in range(basis_count):
                term = radial[pl.ds(part * 64 + b, 8, stride=8), :]
                basis_part = term if basis_part is None else basis_part + term
            alongs = [along[pl.ds(part * 64 + m, 8, stride=8), :] for m in range(4)]
            step = [displace[axis, at, :] for axis in range(3)]
            env_grad = alongs[0] + 0.5 * (
                alongs[1] * step[0] + alongs[2] * step[1] + alongs[3] * step[2]
            )
            square_grad = -basis_part - env_grad * keep_inner[at, :] * (2.0 / cutoff_square)
            half_env = (0.5 * copies) * env_harm[at, :]
            square_grad = scale * square_grad
            at_center = pl.ds(pl.multiple_of(first_row + part * 8, 8), 8)
            for axis in range(3):
                grad = square_grad * step[axis] + half_env * alongs[axis + 1]
                totals[axis] = totals[axis] + grad
                own_sums[center_turn * 3 + axis, at_center, :] += grad
        for axis in range(3):
            neigh_sums[3 * index + axis] += totals[axis]
        return carry

    lax.fori_loop(0, whole_units, functools.partial(run_unit, block), 0)
    if not far:
        lax.fori_loop(whole_units, units, functools.partial(run_unit, rows), 0)
    if not far:
        return

    def column_sums(ref, index):
        return jnp.concatenate(
            [jnp.sum(ref[3 * index + axis], axis=0, keepdims=True) for axis in range(3)], axis=0
        )

    far_out[...] = column_sums(neigh_sums, groups)
    near_out[...] = column_sums(earlier_neigh, groups)
    for turn in range(groups):
        wide = jnp.zeros((block, block), F32)
        for axis in range(3):
            rows_sum = jnp.sum(own_sums[3 * turn + axis], axis=1, keepdims=True)
            wide = jnp.where(lane == axis, rows_sum, wide)
        shares[turn][...] = column_sums(earlier_neigh, turn) - wide.T[0:3, :]


def tiles_call(groups, slots, stage, listed_far, own, side, weights, earlier):
    far = stage == "far"
    latent, block = weights[0].shape
    vmem = pl.BlockSpec(memory_space=pltpu.VMEM)
    smem = pl.BlockSpec(memory_space=pltpu.SMEM)
    heads = ([listed_far] if far else []) + list(own) + ([] if side is None else [side])
    operands = [*heads, *weights, *earlier]
    specs = [vmem] * len(operands)
    sums_shape = (3 * groups, block, block)
    neigh_shape = (3 * (groups + 1), 8, block)
    half_neigh = pltpu.VMEM((groups + 1, latent, block), BF16)
    pos = pltpu.VMEM((groups + 1, 8, block), F32)
    if far:
        results = [jax.ShapeDtypeStruct((3, block), F32)] * (groups + 2)
        results.append(pltpu.VMEM(sums_shape, F32))
        specs[0] = smem
    else:
        shapes = [(8 * groups * block, latent), sums_shape, sums_shape, neigh_shape]
        shapes.append((groups, latent, block))
        results = [pltpu.VMEM(shape, F32) for shape in shapes] + [half_neigh, pos]
    result_specs = [vmem] * len(results)
    first = len(heads) + len(weights)
    aliases = {}
    if far:
        aliases = {first + 2: groups + 2}
    elif stage == "near":
        aliases = {first + n: n for n in range(len(results))}
        results = results + [pltpu.SMEM((1 + 2 * (groups + 1),), jnp.int32)]
        result_specs = result_specs + [smem]

    def body(*refs):
        refs = list(refs)
        take = lambda count: [refs.pop(0) for _ in range(count)]
        listed_ref = take(1)[0] if far else None
        own_refs = take(len(own))
        side_ref = None if side is None else take(1)[0]
        weight_refs = take(3)
        earlier_refs = take(len(earlier))
        result_refs = take(len(results))
        tiles_kernel(
            groups, slots, stage, listed_ref, own_refs, side_ref, weight_refs, earlier_refs,
            result_refs, refs,
        )

    scratch = []
    if far:
        scratch += [half_neigh, pos, pltpu.VMEM(neigh_shape, F32)]
    if stage != "ahead":
        scratch += [
            pltpu.VMEM((block + 8, block), F32),
            pltpu.VMEM((4 * block + 8, block), F32),
            pltpu.VMEM((3, block, block), F32),
            pltpu.VMEM((block, block), F32),
            pltpu.VMEM((8 * block, block), F32),
            pltpu.VMEM((8 * block, block), F32),
        ]
    if stage == "near":
        scratch += [
            pltpu.VMEM((8 * groups, block), jnp.int32),
            pltpu.SMEM((8 * groups, block), jnp.int32),
            pltpu.SemaphoreType.DMA,
            pltpu.SMEM((3 * groups * groups,), jnp.int32),
            pltpu.SMEM((4, groups * groups * (groups + 1) + 1), jnp.int32),
        ]
    tiles = {"ahead": 0, "near": groups * slots // 2, "far": groups * slots // 3}[stage]
    return pl.pallas_call(
        body,
        out_shape=results,
        in_specs=specs,
        out_specs=result_specs,
        input_output_aliases=aliases,
        scratch_shapes=scratch,
        compiler_params=pltpu.CompilerParams(vmem_limit_bytes=32 * 1024 * 1024),
        cost_estimate=pl.CostEstimate(
            flops=(tiles * (block // groups) * 200 + 24 * latent) * block * latent,
            bytes_accessed=sum(x.size * x.dtype.itemsize for x in operands),
            transcendentals=tiles * (block // groups) * block * latent,
        ),
        name=stage + "_tiles",
    )(*operands)


def on_device(
    positions,
    features,
    neighbour_weight,
    adjoint,
    basis_weight,
    edge_weight,
    tile_center,
    tile_neighbour,
    tile_count,
):
    groups = lax.axis_size("grp")
    latent, block = features.shape
    slots = tile_center.shape[0]
    packed_rows = latent + PAD_ROWS
    packed, whole = pl.pallas_call(
        pack_kernel,
        out_shape=[
            pltpu.VMEM((packed_rows, block), BF16),
            pltpu.VMEM((packed_rows + adjoint.shape[0], block), BF16),
        ],
        in_specs=[pl.BlockSpec(memory_space=pl.ANY)] * 6,
        out_specs=[pl.BlockSpec(memory_space=pltpu.VMEM)] * 2,
        scratch_shapes=[
            pltpu.VMEM(positions.shape, F32),
            pltpu.SMEM((2, slots), jnp.int32),
            pltpu.SMEM((1,), jnp.int32),
            pltpu.SemaphoreType.DMA((7,)),
        ],
        name="pack_rows",
    )(positions, features, adjoint, tile_center, tile_neighbour, tile_count)
    own = [whole] + [turned(whole, turn) for turn in range(1, groups)]
    near = swapped(packed, 0)
    far = swapped(packed, 1)
    weights = (neighbour_weight, basis_weight, edge_weight.T)
    ahead = tiles_call(groups, slots, "ahead", None, own[:1], near, weights, [])
    *kept, far_work = tiles_call(groups, slots, "near", None, own, None, weights, ahead)
    *shares, far_sum, near_sum, _ = tiles_call(
        groups, slots, "far", far_work, [], far, weights, kept[:5]
    )
    total = shares[0] + swapped(far_sum, 1) + swapped(near_sum, 0)
    for turn in range(1, groups):
        total = total + turned(shares[turn], -turn)
    return total


def solution(mesh):
    placed = (
        P(None, ("dom", "grp")),
        P(None, ("dom", "grp")),
        P(),
        P(None, ("dom", "grp")),
        P(),
        P(),
        P(("dom", "grp")),
        P(("dom", "grp")),
        P(("dom", "grp")),
    )
    return jax.shard_map(
        on_device, mesh=mesh, in_specs=placed, out_specs=P(None, ("dom", "grp")), check_vma=False
    )
```

```python
import functools
import math

import jax
import jax.numpy as jnp
from jax import lax
from jax.experimental import pallas as pl
from jax.experimental.pallas import tpu as pltpu
from jax.sharding import PartitionSpec as P

slab_length = 1.0
cutoff_square = 4.0
F32 = jnp.float32
BF16 = jnp.bfloat16
COLUMN_STEP = 8
PAD_ROWS = 16


def turned(value, by):
    count = lax.axis_size("grp")
    return lax.ppermute(value, "grp", [((i + by) % count, i) for i in range(count)])


def swapped(value, side):
    count = lax.axis_size("dom")
    pairs = []
    for i in range(0, count, 2):
        other = (i + 1 - 2 * side) % count
        pairs += [(i, other), (other, i)]
    return lax.ppermute(value, "dom", pairs)


def pack_kernel(
    groups, positions, features, adjoint, tile_center, tile_neighbour, tile_count, packed, whole, coords,
    lists, counts, sems,
):
    latent, block = features.shape
    slots = tile_center.shape[0]
    copies = [
        pltpu.make_async_copy(source, target, sems.at[n])
        for n, (source, target) in enumerate(
            [
                (features, packed.at[0:latent]),
                (features, whole.at[0:latent]),
                (adjoint, whole.at[latent + PAD_ROWS : whole.shape[0]]),
                (positions, coords),
                (tile_center, lists.at[0]),
                (tile_neighbour, lists.at[1]),
                (tile_count, counts),
            ]
        )
    ]
    for copy in copies:
        copy.start()
    for copy in copies[3:]:
        copy.wait()
    values = coords[...]
    high = values.astype(BF16).astype(F32)
    rest = values - high
    middle = rest.astype(BF16).astype(F32)
    low = rest - middle
    lane = lax.broadcasted_iota(jnp.int32, (1, block), 1)
    listed = jnp.zeros((1, block), F32)
    for slot in range(slots):
        entry = lists[0, slot] * (3 * groups) + lists[1, slot]
        entry = jnp.where(slot < counts[0], entry, block)
        listed = listed + jnp.where(lane == entry, 1.0, 0.0)
    parts = [high, middle, low, listed, jnp.zeros((PAD_ROWS - 10, block), F32)]
    parts = jnp.concatenate(parts, axis=0).astype(BF16)
    packed[latent : latent + PAD_ROWS, :] = parts
    whole[latent : latent + PAD_ROWS, :] = parts
    for copy in copies[:3]:
        copy.wait()


def tiles_kernel(groups, stage, listed_far, own, side, weights, earlier, results, scratch):
    (neighbour_weight, basis_weight, edge_weight) = weights
    far = stage == "far"
    if far:
        mixed, cols, _, earlier_neigh, half_own = earlier
        *shares, far_out, near_out, own_sums = results
        (half_neigh, pos, neigh_sums, dist, env_harm, displace, keep_inner, radial, along) = scratch
    else:
        mixed, cols, own_sums, neigh_sums, half_own, half_neigh, pos, *far_work = results
        if stage == "near":
            (far_work,) = far_work
            (dist, env_harm, displace, keep_inner, radial, along, tally, work) = scratch
    prepared = {"ahead": range(1), "near": range(1, groups), "far": range(0)}[stage]
    latent, block = neighbour_weight.shape
    basis_count = basis_weight.shape[0]
    channels = edge_weight.shape[0]
    rows = block // groups
    packed_rows = latent + PAD_ROWS
    window = 3 * groups
    member = lax.axis_index("grp")
    near_slab = 2 - 2 * lax.rem(lax.axis_index("dom"), 2)
    far_slab = 2 - near_slab
    side_slab = far_slab if far else near_slab

    if stage == "near":
        listed = sum(
            ref[latent : latent + PAD_ROWS, :].astype(F32)[9:10, :] for ref in own
        )
        lane_row = lax.broadcasted_iota(jnp.int32, (1, block), 1)
        for entry in range(groups * window):
            tally[entry] = jnp.sum(jnp.where(lane_row == entry, listed, 0.0)).astype(jnp.int32)

    third = lax.broadcasted_iota(jnp.int32, (8, block), 0) == 2
    zero5 = jnp.zeros((5, block), F32)

    def coords_of(part):
        return jnp.concatenate([part[0:3] + part[3:6] + part[6:9], zero5], axis=0)

    def neighbour(index, ref, start, lift):
        product = lax.dot_general(
            neighbour_weight[...],
            ref[start : start + latent, :],
            (((0,), (0,)), ((), ())),
            preferred_element_type=F32,
        )
        half_neigh[index] = product.astype(BF16) * 0.5
        part = ref[start + latent : start + packed_rows, :].astype(F32)
        pos[index] = coords_of(part) + jnp.where(third, lift, 0.0)

    lift = jnp.asarray(side_slab - 1, jnp.int32).astype(F32) * slab_length
    if stage != "near":
        neighbour(groups, side, 0, lift)
    for turn in prepared:
        neighbour(turn, own[turn], 0, 0.0)

    sub8 = lax.broadcasted_iota(jnp.int32, (8, block), 0)
    rates = jnp.zeros((8, block), F32)
    for b in range(basis_count):
        rates = jnp.where(sub8 == b, 0.3 * 1.5**b, rates)
    weight_rows = basis_weight[...].astype(F32) * 0.5
    rated_rows = weight_rows * rates
    exponents = rates * (-math.log2(math.e))
    lane = lax.broadcasted_iota(jnp.int32, (latent, block), 1)
    weight_cols = (
        jnp.concatenate([weight_rows, jnp.zeros((block - basis_count, latent), F32)], axis=0)
        .T
    )
    eye = jnp.where(
        lax.broadcasted_iota(jnp.int32, (latent, latent), 0)
        == lax.broadcasted_iota(jnp.int32, (latent, latent), 1),
        1.0,
        0.0,
    ).astype(BF16)
    for turn in prepared:
        half_own[turn] = own[turn][0:latent, :].astype(F32) * 0.5
        own_sums[3 * turn : 3 * turn + 3] = jnp.zeros((3, block, block), F32)
        for m in range(4):
            at = (turn * 8 + m) * block
            mixed[at : at + block, :] = lax.dot_general(
                own[turn][packed_rows + m * channels : packed_rows + (m + 1) * channels, :],
                edge_weight[...],
                (((0,), (0,)), ((), ())),
                preferred_element_type=F32,
            )
            at = (turn * 8 + 4 + m) * block
            mixed[at : at + block, :] = jnp.zeros((block, latent), F32)
        part = own[turn][latent : latent + PAD_ROWS, :].astype(F32)
        column = jnp.concatenate(
            [coords_of(part), jnp.zeros((block - 8, block), F32)], axis=0
        ).T
        for axis in range(3):
            cols[turn * 3 + axis] = jnp.broadcast_to(column[:, axis : axis + 1], (block, block))
    if stage != "near":
        neigh_sums[...] = jnp.zeros_like(neigh_sums)
    if stage == "ahead":
        return

    if not far:
        def copies_of(center, slab, b):
            return tally[center * window + slab * groups + b]

        def live(center, slab, b):
            return jnp.where(copies_of(center, slab, b) > 0, 1, 0)

        pool = sum(live(center, 1, b) for center in range(groups) for b in range(groups))
        fixed = [
            sum(live(center, slab, b) for center in range(groups) for slab in (0, 2))
            for b in range(groups)
        ]
        target = pool + sum(fixed)
        begin, end, edge = jnp.int32(0), jnp.int32(0), jnp.int32(0)
        for b in range(groups):
            following = jnp.minimum(
                edge + jnp.maximum(target - groups * fixed[b], 0), groups * pool
            )
            begin = jnp.where(member == b, edge, begin)
            end = jnp.where(member == b, following, end)
            edge = following
        units = jnp.int32(0)
        for center in range(groups):
            turn = lax.rem(center - member + groups, groups)
            work[0, units] = turn
            work[2, units] = groups
            work[3, units] = copies_of(center, near_slab, member)
            units = units + live(center, near_slab, member)
        whole_units = units
        place = jnp.int32(0)
        for center in range(groups):
            turn = lax.rem(center - member + groups, groups)
            for b in range(groups):
                for part in range(groups):
                    work[0, units] = turn
                    work[1, units] = part
                    work[2, units] = lax.rem(b - member + groups, groups)
                    work[3, units] = copies_of(center, 1, b)
                    mine = jnp.logical_and(place >= begin, place < end)
                    units = units + jnp.where(mine, live(center, 1, b), 0)
                    place = place + live(center, 1, b)
        far_units = jnp.int32(0)
        for center in range(groups):
            far_work[1 + far_units * 2] = lax.rem(center - member + groups, groups)
            far_work[2 + far_units * 2] = copies_of(center, far_slab, member)
            far_units = far_units + live(center, far_slab, member)
        far_work[0] = far_units
    else:
        units = whole_units = listed_far[0]

    def run_unit(rows, unit, carry):
        if far:
            center_turn = listed_far[1 + unit * 2]
            first_row = 0
            copies = listed_far[2 + unit * 2].astype(F32)
            index = groups
            self_pair = jnp.float32(0.0)
        else:
            center_turn = work[0, unit]
            first_row = pl.multiple_of(work[1, unit] * rows, rows) if rows < block else 0
            index = work[2, unit]
            copies = work[3, unit].astype(F32)
            self_pair = jnp.where(center_turn == index, 1.0, 0.0).astype(F32)

        square = None
        steps = []
        for axis in range(3):
            step = (
                pos[index, axis : axis + 1, :]
                - cols[center_turn * 3 + axis, pl.ds(first_row, rows), :]
            )
            steps.append(step)
            square = step * step if square is None else square + step * step
        same = (
            lax.broadcasted_iota(jnp.int32, (rows, block), 0) + first_row
            == lax.broadcasted_iota(jnp.int32, (rows, block), 1)
        )
        keep = 1.0 - self_pair * jnp.where(same, 1.0, 0.0)
        inner = jnp.maximum(1.0 - square * (1.0 / cutoff_square), 0.0) * keep
        envelope = inner * inner
        dist[0:rows, :] = square
        keep_inner[0:rows, :] = inner
        env_harm[0:rows, :] = envelope
        for axis in range(3):
            displace[axis, 0:rows, :] = steps[axis]
            env_harm[(axis + 1) * rows : (axis + 2) * rows, :] = envelope * (steps[axis] * 0.5)
        half_n = half_neigh[index]
        rest = jnp.concatenate([jnp.zeros((block - 2 * basis_count, block), BF16), half_n], axis=0)
        rest = jnp.concatenate([rest, rest], axis=1)
        half_center = half_own[center_turn]

        for chunk in range(rows // COLUMN_STEP):
            first = chunk * COLUMN_STEP
            shift = lax.rem(2 * block - first_row - first + basis_count, block)
            rolled = pltpu.roll(half_center, shift, 1)
            rolled = jnp.where(lane < basis_count, weight_cols, rolled)
            rolled = jnp.where(lane < 2 * basis_count, rolled, 0.0)
            left = jnp.concatenate([rolled.astype(BF16), eye], axis=1)
            for k in range(0, COLUMN_STEP, 2):
                right = []
                basis = []
                for e in (k, k + 1):
                    vals = jnp.exp2(exponents * dist[pl.ds(first + e, 8, stride=0), :])
                    basis.append(vals)
                    onehot = jnp.where(sub8 == e, 1.0, 0.0)
                    right.append(jnp.concatenate([vals, onehot], axis=0).astype(BF16))
                right = jnp.concatenate([jnp.concatenate(right, axis=1), rest], axis=0)
                pre = jnp.dot(left, right, preferred_element_type=F32)
                for n, e in enumerate((k, k + 1)):
                    half = pre[:, n * block : (n + 1) * block].astype(BF16)
                    tanh = jnp.tanh(half)
                    up = 1 + tanh
                    hidden = half * up
                    slope = up + hidden * (1 - tanh)
                    both = jnp.concatenate([slope, hidden], axis=0)
                    row = first + e
                    at = center_turn * (8 * block) + first_row + row
                    mix = [mixed[pl.ds(at + m * block, 8, stride=0), :] for m in range(4)]
                    top = jnp.concatenate([mix[m] * rated_rows for m in range(4)], axis=0)
                    exact = mixed[pl.ds(at, 8, stride=block), :]
                    high = exact.astype(BF16).astype(F32)
                    low = jnp.concatenate([high, exact - high], axis=0)
                    lhs = jnp.concatenate(
                        [
                            jnp.concatenate([top, jnp.zeros((16, latent), F32)], axis=0),
                            jnp.concatenate([jnp.zeros((32, latent), F32), low], axis=0),
                        ],
                        axis=1,
                    ).astype(BF16)
                    out = jnp.dot(lhs, both, preferred_element_type=F32)
                    total = None
                    for m in range(4):
                        at = m * rows + row
                        term = env_harm[pl.ds(at, 8, stride=0), :] * out[m * 8 : m * 8 + 8]
                        total = term if total is None else total + term
                    radial[row * 8 : row * 8 + 8, :] = total * basis[n]
                    along[row * 8 : row * 8 + 8, :] = out[32:40] + out[40:48]

        totals = [jnp.zeros((8, block), F32) for _ in range(3)]
        scale = copies * 2.0
        for part in range(rows // 8):
            at = slice(part * 8, part * 8 + 8)
            basis_part = None
            for b in range(basis_count):
                term = radial[pl.ds(part * 64 + b, 8, stride=8), :]
                basis_part = term if basis_part is None else basis_part + term
            alongs = [along[pl.ds(part * 64 + m, 8, stride=8), :] for m in range(4)]
            step = [displace[axis, at, :] for axis in range(3)]
            env_grad = alongs[0] + 0.5 * (
                alongs[1] * step[0] + alongs[2] * step[1] + alongs[3] * step[2]
            )
            square_grad = -basis_part - env_grad * keep_inner[at, :] * (2.0 / cutoff_square)
            half_env = (0.5 * copies) * env_harm[at, :]
            square_grad = scale * square_grad
            at_center = pl.ds(pl.multiple_of(first_row + part * 8, 8), 8)
            for axis in range(3):
                grad = square_grad * step[axis] + half_env * alongs[axis + 1]
                totals[axis] = totals[axis] + grad
                own_sums[center_turn * 3 + axis, at_center, :] += grad
        for axis in range(3):
            neigh_sums[3 * index + axis] += totals[axis]
        return carry

    lax.fori_loop(0, whole_units, functools.partial(run_unit, block), 0)
    if not far:
        lax.fori_loop(whole_units, units, functools.partial(run_unit, rows), 0)
    if not far:
        return

    def column_sums(ref, index):
        return jnp.concatenate(
            [jnp.sum(ref[3 * index + axis], axis=0, keepdims=True) for axis in range(3)], axis=0
        )

    far_out[...] = column_sums(neigh_sums, groups)
    near_out[...] = column_sums(earlier_neigh, groups)
    for turn in range(groups):
        wide = jnp.zeros((block, block), F32)
        for axis in range(3):
            rows_sum = jnp.sum(own_sums[3 * turn + axis], axis=1, keepdims=True)
            wide = jnp.where(lane == axis, rows_sum, wide)
        shares[turn][...] = column_sums(earlier_neigh, turn) - wide.T[0:3, :]


def tiles_call(groups, slots, stage, listed_far, own, side, weights, earlier):
    far = stage == "far"
    latent, block = weights[0].shape
    vmem = pl.BlockSpec(memory_space=pltpu.VMEM)
    smem = pl.BlockSpec(memory_space=pltpu.SMEM)
    heads = ([listed_far] if far else []) + list(own) + ([] if side is None else [side])
    operands = [*heads, *weights, *earlier]
    specs = [vmem] * len(operands)
    sums_shape = (3 * groups, block, block)
    neigh_shape = (3 * (groups + 1), 8, block)
    half_neigh = pltpu.VMEM((groups + 1, latent, block), BF16)
    pos = pltpu.VMEM((groups + 1, 8, block), F32)
    if far:
        results = [jax.ShapeDtypeStruct((3, block), F32)] * (groups + 2)
        results.append(pltpu.VMEM(sums_shape, F32))
        specs[0] = smem
    else:
        shapes = [(8 * groups * block, latent), sums_shape, sums_shape, neigh_shape]
        shapes.append((groups, latent, block))
        results = [pltpu.VMEM(shape, F32) for shape in shapes] + [half_neigh, pos]
    result_specs = [vmem] * len(results)
    first = len(heads) + len(weights)
    aliases = {}
    if far:
        aliases = {first + 2: groups + 2}
    elif stage == "near":
        aliases = {first + n: n for n in range(len(results))}
        results = results + [pltpu.SMEM((1 + 2 * (groups + 1),), jnp.int32)]
        result_specs = result_specs + [smem]

    def body(*refs):
        refs = list(refs)
        take = lambda count: [refs.pop(0) for _ in range(count)]
        listed_ref = take(1)[0] if far else None
        own_refs = take(len(own))
        side_ref = None if side is None else take(1)[0]
        weight_refs = take(3)
        earlier_refs = take(len(earlier))
        result_refs = take(len(results))
        tiles_kernel(
            groups, stage, listed_ref, own_refs, side_ref, weight_refs, earlier_refs,
            result_refs, refs,
        )

    scratch = []
    if far:
        scratch += [half_neigh, pos, pltpu.VMEM(neigh_shape, F32)]
    if stage != "ahead":
        scratch += [
            pltpu.VMEM((block + 8, block), F32),
            pltpu.VMEM((4 * block + 8, block), F32),
            pltpu.VMEM((3, block, block), F32),
            pltpu.VMEM((block, block), F32),
            pltpu.VMEM((8 * block, block), F32),
            pltpu.VMEM((8 * block, block), F32),
        ]
    if stage == "near":
        scratch += [
            pltpu.SMEM((3 * groups * groups,), jnp.int32),
            pltpu.SMEM((4, groups * groups * (groups + 1) + 1), jnp.int32),
        ]
    tiles = {"ahead": 0, "near": groups * slots // 2, "far": groups * slots // 3}[stage]
    return pl.pallas_call(
        body,
        out_shape=results,
        in_specs=specs,
        out_specs=result_specs,
        input_output_aliases=aliases,
        scratch_shapes=scratch,
        compiler_params=pltpu.CompilerParams(vmem_limit_bytes=32 * 1024 * 1024),
        cost_estimate=pl.CostEstimate(
            flops=(tiles * (block // groups) * 200 + 24 * latent) * block * latent,
            bytes_accessed=sum(x.size * x.dtype.itemsize for x in operands),
            transcendentals=tiles * (block // groups) * block * latent,
        ),
        name=stage + "_tiles",
    )(*operands)


def on_device(
    positions,
    features,
    neighbour_weight,
    adjoint,
    basis_weight,
    edge_weight,
    tile_center,
    tile_neighbour,
    tile_count,
):
    groups = lax.axis_size("grp")
    latent, block = features.shape
    slots = tile_center.shape[0]
    packed_rows = latent + PAD_ROWS
    packed, whole = pl.pallas_call(
        functools.partial(pack_kernel, groups),
        out_shape=[
            pltpu.VMEM((packed_rows, block), BF16),
            pltpu.VMEM((packed_rows + adjoint.shape[0], block), BF16),
        ],
        in_specs=[pl.BlockSpec(memory_space=pl.ANY)] * 6,
        out_specs=[pl.BlockSpec(memory_space=pltpu.VMEM)] * 2,
        scratch_shapes=[
            pltpu.VMEM(positions.shape, F32),
            pltpu.SMEM((2, slots), jnp.int32),
            pltpu.SMEM((1,), jnp.int32),
            pltpu.SemaphoreType.DMA((7,)),
        ],
        name="pack_rows",
    )(positions, features, adjoint, tile_center, tile_neighbour, tile_count)
    own = [whole] + [turned(whole, turn) for turn in range(1, groups)]
    near = swapped(packed, 0)
    far = swapped(packed, 1)
    weights = (neighbour_weight, basis_weight, edge_weight.T)
    ahead = tiles_call(groups, slots, "ahead", None, own[:1], near, weights, [])
    *kept, far_work = tiles_call(groups, slots, "near", None, own, None, weights, ahead)
    *shares, far_sum, near_sum, _ = tiles_call(
        groups, slots, "far", far_work, [], far, weights, kept[:5]
    )
    total = shares[0] + swapped(far_sum, 1) + swapped(near_sum, 0)
    for turn in range(1, groups):
        total = total + turned(shares[turn], -turn)
    return total


def solution(mesh):
    placed = (
        P(None, ("dom", "grp")),
        P(None, ("dom", "grp")),
        P(),
        P(None, ("dom", "grp")),
        P(),
        P(),
        P(("dom", "grp")),
        P(("dom", "grp")),
        P(("dom", "grp")),
    )
    return jax.shard_map(
        on_device, mesh=mesh, in_specs=placed, out_specs=P(None, ("dom", "grp")), check_vma=False
    )
```
